32 devices in a mesh: half: 2 (over x), quarter: 2 (over y), grp: 8 (over z, core).
Axes of the slice: x: 2, y: 2, z: 4, core: 2. Of those that a mesh axis runs over, the one named last changes fastest.
Arguments:
- rhs: float32 [8192, 512], P(('half', 'quarter', 'grp')), may hold values from -6 to 6
- left_one: float32 [8192, 128], P(('half', 'quarter', 'grp')), may hold values from -0.5 to 0.5
- left_two: float32 [8192, 128], P(('half', 'quarter', 'grp')), may hold values from -0.5 to 0.5
- middle_one: float32 [2, 8, 128, 128], P('half', 'grp'), may hold values from -0.5 to 0.5
- middle_two: float32 [4, 8, 128, 128], P(('half', 'quarter'), 'grp'), may hold values from -0.5 to 0.5
- right_one: float32 [8192, 128], P(('half', 'quarter', 'grp')), may hold values from -0.25 to 0.25
- right_two: float32 [8192, 128], P(('half', 'quarter', 'grp')), may hold values from -0.375 to 0.375
- order_one: int32 [2, 8, 8], P('half', 'grp'), may hold values from 0 to 7, each once within a row
- order_two: int32 [4, 8, 8], P(('half', 'quarter'), 'grp'), may hold values from 0 to 7, each once within a row
Outputs:
- product: float32 [8192, 512], P(('half', 'quarter', 'grp'))
The draws below stay inside these ranges and needn't reach their ends.
Inputs may be any that keep to these rules, and one draw needn't show every extreme that they name: `order_one`: each row along the last dimension is a permutation of 0 .. 7. `order_two`: each row along the last dimension is a permutation of 0 .. 7.
All inputs are finite; a program needn't handle non-finite values.
Results may differ from the reference program's by a relative error of at most 0.000071.
Values sent between devices are 32-bit elements; how exact they have to be, the bound alone decides.
No kernel may reach another device: no remote copies, remote signals or barrier semaphores. Data moves between devices by JAX's collectives and lax.ppermute only.
A program may use at most 64 MiB of HBM per device.

```python
import jax
import jax.numpy as jnp
from jax import lax

CR = 256
NRHS = 512
RK = 128
NTOTAL = 8192
N_GRP = 8


def block_levels(stream_key, dims, split, least, largest):
    factor_of = 1.0
    for position, blocks in split:
        heights = jax.random.uniform(jax.random.fold_in(jax.random.fold_in(stream_key, 6), position), (blocks,), jnp.float32, least / len(split), largest / len(split))
        factor_of = factor_of * jnp.repeat(jnp.exp(heights), dims[position] // blocks).reshape((-1,) + (1,) * (len(dims) - 1 - position))
    return factor_of


def scatter_about(stream_key, dims, spread, limit, shards=(), dtype=jnp.bfloat16):
    values = jax.random.normal(stream_key, dims, jnp.float32) * spread
    if len(shards) > 0:
        values = block_levels(stream_key, dims, shards, -0.22, 0.18) * values
    return jnp.clip(values, min=-limit, max=limit).astype(dtype)


def setup_inputs(seed: int = 0) -> dict:
    seeds = jax.random.split(jax.random.key(seed), 10)
    return {
        "rhs": scatter_about(seeds[0], (NTOTAL, NRHS), 1.0, 6.0, ((0, 32),), jnp.float32),
        "left_one": scatter_about(seeds[1], (NTOTAL, RK), RK ** -0.5, 0.5, ((0, 32),), jnp.float32),
        "left_two": scatter_about(seeds[2], (NTOTAL, RK), RK ** -0.5, 0.5, ((0, 32),), jnp.float32),
        "middle_one": scatter_about(seeds[3], (2, N_GRP, RK, RK), RK ** -0.5, 0.5, ((0, 2), (1, 8)), jnp.float32),
        "middle_two": scatter_about(seeds[4], (4, N_GRP, RK, RK), RK ** -0.5, 0.5, ((0, 4), (1, 8)), jnp.float32),
        "right_one": scatter_about(seeds[5], (NTOTAL, RK), (2 * CR) ** -0.5, 0.25, ((0, 32),), jnp.float32),
        "right_two": scatter_about(seeds[6], (NTOTAL, RK), CR ** -0.5, 0.375, ((0, 32),), jnp.float32),
        "order_one": jax.vmap(lambda own: jax.random.permutation(own, N_GRP))(jax.random.split(seeds[7], 2 * N_GRP)).reshape((2, N_GRP, N_GRP)).astype(jnp.int32),
        "order_two": jax.vmap(lambda own: jax.random.permutation(own, N_GRP))(jax.random.split(seeds[8], 4 * N_GRP)).reshape((4, N_GRP, N_GRP)).astype(jnp.int32),
    }


def regroup(coeffs, order):
    groups = N_GRP
    part = RK // groups
    lead = coeffs.shape[:-2]
    parts = coeffs.reshape(lead + (groups, part, NRHS))
    inverse = jnp.argsort(order, axis=-1).astype(jnp.int32)
    index = jnp.broadcast_to(inverse[..., None, None], parts.shape)
    picked = jnp.take_along_axis(parts, index, axis=-3)
    moved = jnp.swapaxes(picked, -4, -3)
    return moved.reshape(coeffs.shape)


def reference(rhs, left_one, left_two, middle_one, middle_two, right_one, right_two, order_one, order_two):
    highest = lax.Precision.HIGHEST
    groups = N_GRP
    blocks = rhs.reshape(2, 2, groups, CR, NRHS)
    coeff_two = jnp.einsum('abgrk,abgrn->abgkn', right_two.reshape(2, 2, groups, CR, RK), blocks, precision=highest)
    moved_two = regroup(coeff_two, order_two.reshape(2, 2, groups, groups))[:, ::-1]
    mixed_two = jnp.einsum('abgkl,abgln->abgkn', middle_two.reshape(2, 2, groups, RK, RK), moved_two, precision=highest)
    result_two = jnp.einsum('abgrk,abgkn->abgrn', left_two.reshape(2, 2, groups, CR, RK), mixed_two, precision=highest)
    coeff_one = jnp.einsum('aqgrk,aqgrn->agkn', right_one.reshape(2, 2, groups, CR, RK), blocks, precision=highest)
    moved_one = regroup(coeff_one, order_one)[::-1]
    mixed_one = jnp.einsum('agkl,agln->agkn', middle_one, moved_one, precision=highest)
    result_one = jnp.einsum('aqgrk,agkn->aqgrn', left_one.reshape(2, 2, groups, CR, RK), mixed_one, precision=highest)
    return (result_one + result_two).reshape(NTOTAL, NRHS)
```

```python
import functools

import jax
import jax.numpy as jnp
from jax import lax
from jax.experimental import pallas as pl
from jax.experimental.pallas import tpu as pltpu
from jax.sharding import PartitionSpec as P

AXES = ("half", "quarter", "grp")
MOST_CHIPS = 8
PARAMS = pltpu.CompilerParams(vmem_limit_bytes=16 * 2**20)
VMEM = pl.BlockSpec(memory_space=pltpu.VMEM)
SMEM = pl.BlockSpec(memory_space=pltpu.SMEM)


def f32(*shape):
    return jax.ShapeDtypeStruct(shape, jnp.float32)


def split(value):
    high = value.astype(jnp.bfloat16)
    low = (value - high.astype(jnp.float32)).astype(jnp.bfloat16)
    return high, low


def product(left, right, dims=((1,), (0,))):
    dot = functools.partial(
        lax.dot_general,
        dimension_numbers=(dims, ((), ())),
        preferred_element_type=jnp.float32,
    )
    (lh, ll), (rh, rl) = split(left), split(right)
    return dot(lh, rh) + (dot(lh, rl) + dot(ll, rh))


def coefficients(rhs, right_one, right_two):
    both = jnp.concatenate([right_one[...], right_two[...]], axis=1)
    return product(both, rhs[...], ((0,), (0,)))


def project_near(order_one, order_two, rhs, right_one, right_two, own, other, slots):
    me = lax.axis_index("grp")
    coeffs = coefficients(rhs, right_one, right_two)
    part = slots.shape[3]
    for level, order in enumerate((order_one, order_two)):
        for p in range(order.shape[2]):
            apart = order[0, 0, p] ^ me
            first = level * right_one.shape[1] + p * part
            slots[apart & 1, level, apart >> 1] = coeffs[first : first + part]
    own[...] = slots[0]
    other[...] = slots[1]


def project_far(order_one, order_two, rhs, right_one, right_two, slots_one, slots_two):
    coeffs = coefficients(rhs, right_one, right_two)
    part = slots_one.shape[1]
    for level, (order, slots) in enumerate(((order_one, slots_one), (order_two, slots_two))):
        for p in range(order.shape[2]):
            first = level * right_one.shape[1] + p * part
            slots[order[0, 0, p]] = coeffs[first : first + part]


def pair_up(own, sibling, *messages):
    chips = own.shape[1]
    for level in range(own.shape[0]):
        for apart in range(chips):
            message = messages[level * chips + apart]
            message[0] = own[level, apart]
            message[1] = sibling[level, apart]


def outer_factors(left_one, middle_one, left_two, middle_two, factors):
    rank = left_one.shape[1]
    factors[:, :rank] = product(left_one[...], middle_one[0, 0])
    factors[:, rank:] = product(left_two[...], middle_two[0, 0])


def combine(chips, factors, *refs):
    pieces, (out, stacked) = refs[:-2], refs[-2:]
    me = lax.axis_index("grp")
    rank = factors.shape[1] // 2
    part = pieces[0].shape[1]
    for apart in range(chips):
        straight, diagonal, second = (pieces[n * chips + apart] for n in range(3))
        for core in range(2):
            row = pl.multiple_of((me ^ (2 * apart + core)) * part, part)
            stacked[pl.ds(row, part)] = straight[core] + diagonal[core]
            stacked[pl.ds(rank + row, part)] = second[core]
    out[...] = product(factors[...], stacked[...])


def near(mesh, rhs, left_one, left_two, middle_one, middle_two, right_one, right_two, order_one, order_two):
    groups = mesh.shape["grp"]
    chips = groups // 2
    rank, columns = right_one.shape[1], rhs.shape[1]
    part = rank // groups

    def send(value, half=0, quarter=0, grp=0):
        sizes = [mesh.shape[axis] for axis in AXES]
        pairs = []
        for h in range(sizes[0]):
            for q in range(sizes[1]):
                for g in range(sizes[2]):
                    source = (h * sizes[1] + q) * sizes[2] + g
                    target = ((h ^ half) * sizes[1] + (q ^ quarter)) * sizes[2] + (g ^ grp)
                    pairs.append((source, target))
        return lax.ppermute(value, AXES, pairs)

    own, other = pl.pallas_call(
        project_near,
        out_shape=[f32(2, chips, part, columns)] * 2,
        in_specs=[SMEM, SMEM, VMEM, VMEM, VMEM],
        out_specs=[VMEM, VMEM],
        scratch_shapes=[pltpu.VMEM((2, 2, chips, part, columns), jnp.float32)],
        compiler_params=PARAMS,
    )(order_one, order_two, rhs, right_one, right_two)
    factors = pl.pallas_call(
        outer_factors,
        out_shape=f32(left_one.shape[0], 2 * rank),
        in_specs=[VMEM] * 4,
        out_specs=VMEM,
        compiler_params=PARAMS,
    )(left_one, middle_one, left_two, middle_two)
    sibling = send(other, grp=1)
    messages = pl.pallas_call(
        pair_up,
        out_shape=[f32(2, part, columns)] * (2 * chips),
        in_specs=[VMEM, VMEM],
        out_specs=[VMEM] * (2 * chips),
        compiler_params=PARAMS,
    )(own, sibling)
    straight = [send(messages[k], half=1, grp=2 * k) for k in range(chips)]
    second = [send(messages[chips + k], quarter=1, grp=2 * k) for k in range(chips)]
    diagonal = [send(value, quarter=1) for value in straight]
    return pl.pallas_call(
        functools.partial(combine, chips),
        out_shape=f32(left_one.shape[0], columns),
        in_specs=[VMEM] * (1 + 3 * chips),
        out_specs=VMEM,
        scratch_shapes=[pltpu.VMEM((2 * rank, columns), jnp.float32)],
        compiler_params=PARAMS,
    )(factors, *straight, *diagonal, *second)


def far(mesh, rhs, left_one, left_two, middle_one, middle_two, right_one, right_two, order_one, order_two):
    groups = mesh.shape["grp"]
    rank, columns = right_one.shape[1], rhs.shape[1]
    slots = pl.pallas_call(
        project_far,
        out_shape=[f32(groups, rank // groups, columns)] * 2,
        in_specs=[SMEM, SMEM, VMEM, VMEM, VMEM],
        out_specs=[VMEM, VMEM],
        compiler_params=PARAMS,
    )(order_one, order_two, rhs, right_one, right_two)
    swap = [(0, 1), (1, 0)]
    first, second = (
        lax.all_to_all(value, "grp", 0, 0, tiled=True).reshape(rank, columns) for value in slots
    )
    first = lax.ppermute(first, "half", swap)
    first = first + lax.ppermute(first, "quarter", swap)
    second = lax.ppermute(second, "quarter", swap)
    dot = functools.partial(jnp.dot, precision=lax.Precision.HIGHEST)
    result = dot(left_one, dot(middle_one[0, 0], first))
    return result + dot(left_two, dot(middle_two[0, 0], second))


def solution(mesh):
    in_specs = (
        P(AXES, None),
        P(AXES, None),
        P(AXES, None),
        P("half", "grp", None, None),
        P(("half", "quarter"), "grp", None, None),
        P(AXES, None),
        P(AXES, None),
        P("half", "grp", None),
        P(("half", "quarter"), "grp", None),
    )
    groups = mesh.shape["grp"]
    direct = groups % 2 == 0 and groups & (groups - 1) == 0 and groups // 2 <= MOST_CHIPS
    return jax.shard_map(
        functools.partial(near if direct else far, mesh),
        mesh=mesh,
        in_specs=in_specs,
        out_specs=P(AXES, None),
        check_vma=False,
    )
```

```python
import functools

import jax
import jax.numpy as jnp
from jax import lax
from jax.experimental import pallas as pl
from jax.experimental.pallas import tpu as pltpu
from jax.sharding import PartitionSpec as P

AXES = ("half", "quarter", "grp")
MOST_CHIPS = 8
PARAMS = pltpu.CompilerParams(vmem_limit_bytes=16 * 2**20)
VMEM = pl.BlockSpec(memory_space=pltpu.VMEM)
HBM = pl.BlockSpec(memory_space=pltpu.HBM)
SMEM = pl.BlockSpec(memory_space=pltpu.SMEM)


def f32(*shape):
    return jax.ShapeDtypeStruct(shape, jnp.float32)


def in_hbm(value):
    return pltpu.with_memory_space_constraint(value, pltpu.HBM)


def split(value):
    high = value.astype(jnp.bfloat16)
    low = (value - high.astype(jnp.float32)).astype(jnp.bfloat16)
    return high, low


def product(left, right, dims=((1,), (0,))):
    dot = functools.partial(
        lax.dot_general,
        dimension_numbers=(dims, ((), ())),
        preferred_element_type=jnp.float32,
    )
    (lh, ll), (rh, rl) = split(left), split(right)
    return dot(lh, rh) + (dot(lh, rl) + dot(ll, rh))


def project_one(
    order_one, order_two, rhs, right_one, right_two,
    own, other, rhs_here, right_here, order_here,
    slots, right, orders, sems,
):
    copies = [
        pltpu.make_async_copy(*pair, sems.at[n])
        for n, pair in enumerate(
            (
                (right_one, right),
                (rhs, rhs_here),
                (order_one, orders),
                (right_two, right_here),
                (order_two, order_here),
            )
        )
    ]
    for copy in copies:
        copy.start()
    me = lax.axis_index("grp")
    for copy in copies[:3]:
        copy.wait()
    coeffs = product(right[...], rhs_here[...], ((0,), (0,)))
    part = slots.shape[2]
    for p in range(orders.shape[2]):
        apart = orders[0, 0, p] ^ me
        slots[apart & 1, apart >> 1] = coeffs[p * part : (p + 1) * part]
    own[...] = slots[0]
    other[...] = slots[1]
    for copy in copies[3:]:
        copy.wait()


def project_two(order, rhs, right, own, other, slots):
    me = lax.axis_index("grp")
    coeffs = product(right[...], rhs[...], ((0,), (0,)))
    part = slots.shape[3]
    for p in range(order.shape[2]):
        receiver = order[0, 0, p]
        apart = (receiver >> 1) ^ (me >> 1)
        slots[(apart ^ me) & 1, apart >> 1, receiver & 1] = coeffs[p * part : (p + 1) * part]
    own[...] = slots[0]
    other[...] = slots[1]


def pair_one(own, sibling, *messages):
    for apart, message in enumerate(messages):
        message[0] = own[apart]
        message[1] = sibling[apart]


def pair_two(own, sibling, *messages):
    for n, message in enumerate(messages):
        message[0] = own[n]
        message[1] = sibling[n]


def pack(*refs):
    out = refs[-1]
    for n, ref in enumerate(refs[:-1]):
        out[n] = ref[...]


def pack_other(*refs):
    out = refs[-1]
    there = 1 - (lax.axis_index("grp") & 1)
    for n, ref in enumerate(refs[:-1]):
        out[n] = ref[:, there]


def outer_factors(left_one, middle_one, left_two, middle_two, factors):
    rank = left_one.shape[1]
    factors[:, :rank] = product(left_one[...], middle_one[0, 0])
    factors[:, rank:] = product(left_two[...], middle_two[0, 0])


def combine(chips, factors, *refs):
    straight, refs = refs[:chips], refs[chips:]
    diagonal, refs = refs[:2], refs[2:]
    second, refs = refs[: chips // 2], refs[chips // 2 :]
    sibling, out, stacked = refs
    me = lax.axis_index("grp")
    core = me & 1
    rank = factors.shape[1] // 2
    part = sibling.shape[2]

    def put(group, level, rows):
        stacked[pl.ds(pl.multiple_of(level * rank + group * part, part), part)] = rows

    for apart in range(chips):
        for other in range(2):
            rows = straight[apart][other] + diagonal[apart // (chips // 2)][apart % (chips // 2), other]
            put(me ^ (2 * apart + other), 0, rows)
    for n in range(chips // 2):
        for other in range(2):
            put(me ^ (2 * (2 * n + core) + other), 1, second[n][other, core])
            put(me ^ (2 * (2 * n + 1 - core) + 1 - other), 1, sibling[n, other])
    out[...] = product(factors[...], stacked[...])


def near(mesh, rhs, left_one, left_two, middle_one, middle_two, right_one, right_two, order_one, order_two):
    groups = mesh.shape["grp"]
    chips = groups // 2
    rank, columns = right_one.shape[1], rhs.shape[1]
    part = rank // groups
    call = functools.partial(pl.pallas_call, compiler_params=PARAMS)

    def send(value, half=0, quarter=0, grp=lambda g: g):
        sizes = [mesh.shape[axis] for axis in AXES]
        pairs = []
        for h in range(sizes[0]):
            for q in range(sizes[1]):
                for g in range(sizes[2]):
                    source = (h * sizes[1] + q) * sizes[2] + g
                    target = ((h ^ half) * sizes[1] + (q ^ quarter)) * sizes[2] + grp(g)
                    pairs.append((source, target))
        return lax.ppermute(value, AXES, pairs)

    own_one, other_one, rhs_here, right_here, order_here = call(
        project_one,
        out_shape=[
            f32(chips, part, columns),
            f32(chips, part, columns),
            rhs,
            right_two,
            order_two,
        ],
        in_specs=[HBM] * 5,
        out_specs=[VMEM] * 4 + [SMEM],
        scratch_shapes=[
            pltpu.VMEM((2, chips, part, columns), jnp.float32),
            pltpu.VMEM(right_one.shape, jnp.float32),
            pltpu.SMEM(order_one.shape, jnp.int32),
            pltpu.SemaphoreType.DMA((5,)),
        ],
    )(*(in_hbm(x) for x in (order_one, order_two, rhs, right_one, right_two)))
    sibling_one = send(other_one, grp=lambda g: g ^ 1)
    own_two, other_two = call(
        project_two,
        out_shape=[f32(chips // 2, 2, part, columns)] * 2,
        in_specs=[SMEM, VMEM, VMEM],
        out_specs=[VMEM, VMEM],
        scratch_shapes=[pltpu.VMEM((2, chips // 2, 2, part, columns), jnp.float32)],
    )(order_here, rhs_here, right_here)
    sibling_two = send(other_two, grp=lambda g: g ^ 1)
    messages_one = call(
        pair_one,
        out_shape=[f32(2, part, columns)] * chips,
        in_specs=[VMEM, VMEM],
        out_specs=[VMEM] * chips,
    )(own_one, sibling_one)
    straight = [send(messages_one[k], half=1, grp=lambda g, k=k: g ^ (2 * k)) for k in range(chips)]
    messages_two = call(
        pair_two,
        out_shape=[f32(2, 2, part, columns)] * (chips // 2),
        in_specs=[VMEM, VMEM],
        out_specs=[VMEM] * (chips // 2),
    )(own_two, sibling_two)
    second = [
        send(messages_two[n], quarter=1, grp=lambda g, n=n: g ^ (2 * (2 * n + (g & 1))))
        for n in range(chips // 2)
    ]
    diagonal = []
    for first in (0, chips // 2):
        packed = call(
            pack,
            out_shape=f32(chips // 2, 2, part, columns),
            in_specs=[VMEM] * (chips // 2),
            out_specs=VMEM,
        )(*straight[first : first + chips // 2])
        diagonal.append(send(packed, quarter=1))
    other_second = call(
        pack_other,
        out_shape=f32(chips // 2, 2, part, columns),
        in_specs=[VMEM] * (chips // 2),
        out_specs=VMEM,
    )(*second)
    sibling_second = send(other_second, grp=lambda g: g ^ 1)
    factors = call(
        outer_factors,
        out_shape=f32(left_one.shape[0], 2 * rank),
        in_specs=[VMEM] * 4,
        out_specs=VMEM,
    )(left_one, middle_one, left_two, middle_two)
    return call(
        functools.partial(combine, chips),
        out_shape=f32(left_one.shape[0], columns),
        in_specs=[VMEM] * (4 + chips + chips // 2),
        out_specs=VMEM,
        scratch_shapes=[pltpu.VMEM((2 * rank, columns), jnp.float32)],
    )(factors, *straight, *diagonal, *second, sibling_second)


def project_far(order_one, order_two, rhs, right_one, right_two, slots_one, slots_two):
    part = slots_one.shape[1]
    levels = ((order_one, right_one, slots_one), (order_two, right_two, slots_two))
    for order, right, slots in levels:
        coeffs = product(right[...], rhs[...], ((0,), (0,)))
        for p in range(order.shape[2]):
            slots[order[0, 0, p]] = coeffs[p * part : (p + 1) * part]


def far(mesh, rhs, left_one, left_two, middle_one, middle_two, right_one, right_two, order_one, order_two):
    groups = mesh.shape["grp"]
    rank, columns = right_one.shape[1], rhs.shape[1]
    slots = pl.pallas_call(
        project_far,
        out_shape=[f32(groups, rank // groups, columns)] * 2,
        in_specs=[SMEM, SMEM, VMEM, VMEM, VMEM],
        out_specs=[VMEM, VMEM],
        compiler_params=PARAMS,
    )(order_one, order_two, rhs, right_one, right_two)
    swap = [(0, 1), (1, 0)]
    first, second = (
        lax.all_to_all(value, "grp", 0, 0, tiled=True).reshape(rank, columns) for value in slots
    )
    first = lax.ppermute(first, "half", swap)
    first = first + lax.ppermute(first, "quarter", swap)
    second = lax.ppermute(second, "quarter", swap)
    dot = functools.partial(jnp.dot, precision=lax.Precision.HIGHEST)
    result = dot(left_one, dot(middle_one[0, 0], first))
    return result + dot(left_two, dot(middle_two[0, 0], second))


def solution(mesh):
    in_specs = (
        P(AXES, None),
        P(AXES, None),
        P(AXES, None),
        P("half", "grp", None, None),
        P(("half", "quarter"), "grp", None, None),
        P(AXES, None),
        P(AXES, None),
        P("half", "grp", None),
        P(("half", "quarter"), "grp", None),
    )
    groups = mesh.shape["grp"]
    direct = groups >= 4 and groups & (groups - 1) == 0 and groups // 2 <= MOST_CHIPS
    return jax.shard_map(
        functools.partial(near if direct else far, mesh),
        mesh=mesh,
        in_specs=in_specs,
        out_specs=P(AXES, None),
        check_vma=False,
    )
```

```python
import functools

import jax
import jax.numpy as jnp
from jax import lax
from jax.experimental import pallas as pl
from jax.experimental.pallas import tpu as pltpu
from jax.sharding import PartitionSpec as P

AXES = ("half", "quarter", "grp")
MOST_CHIPS = 8
COST = 10**10
PARAMS = pltpu.CompilerParams(vmem_limit_bytes=16 * 2**20)
VMEM = pl.BlockSpec(memory_space=pltpu.VMEM)
ANY = pl.BlockSpec(memory_space=pl.ANY)
HBM = pl.BlockSpec(memory_space=pltpu.HBM)
SMEM = pl.BlockSpec(memory_space=pltpu.SMEM)


def f32(*shape):
    return jax.ShapeDtypeStruct(shape, jnp.float32)


def in_hbm(value):
    return pltpu.with_memory_space_constraint(value, pltpu.HBM)


def split(value):
    high = value.astype(jnp.bfloat16)
    low = (value - high.astype(jnp.float32)).astype(jnp.bfloat16)
    return high, low


def product(left, right, dims=((1,), (0,))):
    dot = functools.partial(
        lax.dot_general,
        dimension_numbers=(dims, ((), ())),
        preferred_element_type=jnp.float32,
    )
    (lh, ll), (rh, rl) = split(left), split(right)
    return dot(lh, rh) + (dot(lh, rl) + dot(ll, rh))


def project(
    order_one, order_two, rhs, right_one, right_two,
    kept_one, swapped_one, across_one, diagonal_one, kept_two, swapped_two,
    values, rights, slots_one, slots_two, orders, sems,
):
    rank = right_one.shape[1]
    pairs = (
        (right_one, rights.at[:, :rank]),
        (right_two, rights.at[:, rank:]),
        (rhs, values),
        (order_one, orders.at[0]),
        (order_two, orders.at[1]),
    )
    copies = [pltpu.make_async_copy(*pair, sems.at[n]) for n, pair in enumerate(pairs)]
    for copy in copies:
        copy.start()
    me = lax.axis_index("grp")
    quarter = lax.axis_index("quarter")
    for copy in copies:
        copy.wait()
    coeffs = product(rights[...], values[...], ((0,), (0,)))
    part = kept_one.shape[1]
    for p in range(rank // part):
        first, second = (coeffs[n * rank + p * part : n * rank + (p + 1) * part] for n in range(2))
        apart = orders[0, 0, 0, p] ^ me
        slots_one[((apart >> 1) ^ quarter) & 1, apart & 1, apart >> 2] = first
        receiver = orders[1, 0, 0, p]
        apart = (receiver >> 1) ^ (me >> 1)
        slots_two[(apart ^ me) & 1, apart >> 1, receiver & 1] = second
    kept_one[...] = slots_one[0, 0]
    swapped_one[...] = slots_one[0, 1]
    across_one[...] = slots_one[1, 0]
    diagonal_one[...] = slots_one[1, 1]
    kept_two[...] = slots_two[0]
    swapped_two[...] = slots_two[1]


def add_up(kept, swapped, across, diagonal, *messages):
    for n, message in enumerate(messages):
        message[0] = kept[n] + across[n]
        message[1] = swapped[n] + diagonal[n]


def pair_up(kept, swapped, *messages):
    for n, message in enumerate(messages):
        message[0] = kept[n]
        message[1] = swapped[n]


def pack_other(*refs):
    out = refs[-1]
    there = 1 - (lax.axis_index("grp") & 1)
    for n, ref in enumerate(refs[:-1]):
        out[n] = ref[:, there]


def outer_factors(left_one, middle_one, left_two, middle_two, factors):
    rank = left_one.shape[1]
    factors[:, :rank] = product(left_one[...], middle_one[0, 0])
    factors[:, rank:] = product(left_two[...], middle_two[0, 0])


def put(stacked, apart, rows):
    row = pl.multiple_of((lax.axis_index("grp") ^ apart) * rows.shape[0], rows.shape[0])
    stacked[pl.ds(row, rows.shape[0])] = rows


def regroup_one(*refs):
    stacked = refs[-1]
    half = (len(refs) - 1) // 2
    quarter = lax.axis_index("quarter")
    for n in range(half):
        for other in range(2):
            put(stacked, 4 * n + 2 * quarter + other, refs[n][other])
            put(stacked, 4 * n + 2 * (1 - quarter) + other, refs[half + n][other])


def combine(factors, first, other_second, *refs):
    second, (out, stacked) = refs[:-2], refs[-2:]
    core = lax.axis_index("grp") & 1
    for n in range(len(second)):
        for other in range(2):
            put(stacked, 4 * n + 2 * core + other, second[n][other, core])
            put(stacked, 4 * n + 2 * (1 - core) + 1 - other, other_second[n, other])
    rank = first.shape[0]
    out[...] = product(factors[:, :rank], first[...]) + product(factors[:, rank:], stacked[...])


def near(mesh, rhs, left_one, left_two, middle_one, middle_two, right_one, right_two, order_one, order_two):
    groups = mesh.shape["grp"]
    chips = groups // 2
    half = chips // 2
    rank, columns = right_one.shape[1], rhs.shape[1]
    part = rank // groups

    def call(kernel, out_shape, *operands, after=(), cost=None, scratch=()):
        taken = len(operands)

        def body(*refs):
            kernel(*refs[:taken], *refs[taken + len(after) :])

        return pl.pallas_call(
            body,
            out_shape=out_shape,
            in_specs=[HBM if kernel is project else VMEM] * taken + [ANY] * len(after),
            out_specs=jax.tree.map(lambda _: VMEM, out_shape),
            scratch_shapes=scratch,
            compiler_params=PARAMS,
            cost_estimate=cost and pl.CostEstimate(flops=cost, bytes_accessed=cost // 100, transcendentals=0),
        )(*operands, *after)

    def send(value, to):
        sizes = [mesh.shape[axis] for axis in AXES]
        pairs = []
        for h in range(sizes[0]):
            for q in range(sizes[1]):
                for g in range(sizes[2]):
                    a, b, c = to(h, q, g)
                    source = (h * sizes[1] + q) * sizes[2] + g
                    pairs.append((source, (a * sizes[1] + b) * sizes[2] + c))
        return lax.ppermute(value, AXES, pairs)

    def swap_cores(value):
        return send(value, lambda h, q, g: (h, q, g ^ 1))

    def swap_quarters(value):
        return send(value, lambda h, q, g: (h, 1 - q, g))

    kept_one, swapped_one, across_one, diagonal_one, kept_two, swapped_two = call(
        project,
        [f32(half, part, columns)] * 4 + [f32(half, 2, part, columns)] * 2,
        *(in_hbm(value) for value in (order_one, order_two, rhs, right_one, right_two)),
        scratch=[
            pltpu.VMEM(rhs.shape, jnp.float32),
            pltpu.VMEM((right_one.shape[0], 2 * rank), jnp.float32),
            pltpu.VMEM((2, 2, half, part, columns), jnp.float32),
            pltpu.VMEM((2, half, 2, part, columns), jnp.float32),
            pltpu.SMEM((2, *order_one.shape), jnp.int32),
            pltpu.SemaphoreType.DMA((5,)),
        ],
    )
    across_one = swap_quarters(across_one)
    diagonal_one = send(diagonal_one, lambda h, q, g: (h, 1 - q, g ^ 1))
    swapped_two = swap_cores(swapped_two)
    swapped_one = swap_cores(swapped_one)
    messages_two = call(pair_up, [f32(2, 2, part, columns)] * half, kept_two, swapped_two, after=(swapped_one,))
    second = [
        send(messages_two[n], lambda h, q, g, n=n: (h, 1 - q, g ^ (2 * (2 * n + (g & 1)))))
        for n in range(half)
    ]
    messages_one = call(
        add_up, [f32(2, part, columns)] * half, kept_one, swapped_one, across_one, diagonal_one, after=(messages_two[0],), cost=COST
    )
    first = [
        send(messages_one[n], lambda h, q, g, n=n: (1 - h, q, g ^ (2 * (2 * n + q))))
        for n in range(half)
    ]
    other_first = [swap_quarters(value) for value in first]
    other_second = swap_cores(call(pack_other, f32(half, 2, part, columns), *second))
    factors = call(
        outer_factors, f32(left_one.shape[0], 2 * rank), left_one, middle_one, left_two, middle_two
    )
    stacked = call(regroup_one, f32(rank, columns), *first, *other_first, cost=COST)
    return call(
        combine,
        f32(left_one.shape[0], columns),
        *(factors, stacked, other_second, *second),
        scratch=[pltpu.VMEM((rank, columns), jnp.float32)],
    )


def project_far(order_one, order_two, rhs, right_one, right_two, slots_one, slots_two):
    part = slots_one.shape[1]
    levels = ((order_one, right_one, slots_one), (order_two, right_two, slots_two))
    for order, right, slots in levels:
        coeffs = product(right[...], rhs[...], ((0,), (0,)))
        for p in range(order.shape[2]):
            slots[order[0, 0, p]] = coeffs[p * part : (p + 1) * part]


def far(mesh, rhs, left_one, left_two, middle_one, middle_two, right_one, right_two, order_one, order_two):
    groups = mesh.shape["grp"]
    rank, columns = right_one.shape[1], rhs.shape[1]
    slots = pl.pallas_call(
        project_far,
        out_shape=[f32(groups, rank // groups, columns)] * 2,
        in_specs=[SMEM, SMEM, VMEM, VMEM, VMEM],
        out_specs=[VMEM, VMEM],
        compiler_params=PARAMS,
    )(order_one, order_two, rhs, right_one, right_two)
    swap = [(0, 1), (1, 0)]
    first, second = (
        lax.all_to_all(value, "grp", 0, 0, tiled=True).reshape(rank, columns) for value in slots
    )
    first = lax.ppermute(first, "half", swap)
    first = first + lax.ppermute(first, "quarter", swap)
    second = lax.ppermute(second, "quarter", swap)
    dot = functools.partial(jnp.dot, precision=lax.Precision.HIGHEST)
    result = dot(left_one, dot(middle_one[0, 0], first))
    return result + dot(left_two, dot(middle_two[0, 0], second))


def solution(mesh):
    in_specs = (
        P(AXES, None),
        P(AXES, None),
        P(AXES, None),
        P("half", "grp", None, None),
        P(("half", "quarter"), "grp", None, None),
        P(AXES, None),
        P(AXES, None),
        P("half", "grp", None),
        P(("half", "quarter"), "grp", None),
    )
    groups = mesh.shape["grp"]
    direct = groups >= 4 and groups & (groups - 1) == 0 and groups // 2 <= MOST_CHIPS
    return jax.shard_map(
        functools.partial(near if direct else far, mesh),
        mesh=mesh,
        in_specs=in_specs,
        out_specs=P(AXES, None),
        check_vma=False,
    )
```

```python
import functools

import jax
import jax.numpy as jnp
from jax import lax
from jax.experimental import pallas as pl
from jax.experimental.pallas import tpu as pltpu
from jax.sharding import PartitionSpec as P

AXES = ("half", "quarter", "grp")
MOST_CHIPS = 8
COST = 10**10
PARAMS = pltpu.CompilerParams(vmem_limit_bytes=16 * 2**20)
VMEM = pl.BlockSpec(memory_space=pltpu.VMEM)
ANY = pl.BlockSpec(memory_space=pl.ANY)
HBM = pl.BlockSpec(memory_space=pltpu.HBM)
SMEM = pl.BlockSpec(memory_space=pltpu.SMEM)


def f32(*shape):
    return jax.ShapeDtypeStruct(shape, jnp.float32)


def in_hbm(value):
    return pltpu.with_memory_space_constraint(value, pltpu.HBM)


def split(value):
    high = value.astype(jnp.bfloat16)
    low = (value - high.astype(jnp.float32)).astype(jnp.bfloat16)
    return high, low


def product(left, right, dims=((1,), (0,))):
    dot = functools.partial(
        lax.dot_general,
        dimension_numbers=(dims, ((), ())),
        preferred_element_type=jnp.float32,
    )
    (lh, ll), (rh, rl) = split(left), split(right)
    return dot(lh, rh) + (dot(lh, rl) + dot(ll, rh))


def project(
    order_one, order_two, rhs, right_one, right_two,
    kept_one, swapped_one, across_one, diagonal_one, kept_two, swapped_two,
    values, rights, slots_one, slots_two, orders, sems,
):
    rank = right_one.shape[1]
    pairs = (
        (right_one, rights.at[:, :rank]),
        (right_two, rights.at[:, rank:]),
        (rhs, values),
        (order_one, orders.at[0]),
        (order_two, orders.at[1]),
    )
    copies = [pltpu.make_async_copy(*pair, sems.at[n]) for n, pair in enumerate(pairs)]
    for copy in copies:
        copy.start()
    me = lax.axis_index("grp")
    quarter = lax.axis_index("quarter")
    for copy in copies:
        copy.wait()
    coeffs = product(rights[...], values[...], ((0,), (0,)))
    part = slots_one.shape[4]
    for p in range(rank // part):
        first, second = (coeffs[n * rank + p * part : n * rank + (p + 1) * part] for n in range(2))
        receiver = orders[0, 0, 0, p]
        apart = (receiver >> 1) ^ (me >> 1)
        core = ((apart >> 1) ^ me) & 1
        slots_one[core, (apart ^ quarter) & 1, apart >> 2, receiver & 1] = first
        receiver = orders[1, 0, 0, p]
        apart = (receiver >> 1) ^ (me >> 1)
        slots_two[(apart ^ me) & 1, apart >> 1, receiver & 1] = second
    kept_one[...] = slots_one[0, 0]
    swapped_one[...] = slots_one[1, 0]
    across_one[...] = slots_one[0, 1]
    diagonal_one[...] = slots_one[1, 1]
    kept_two[...] = slots_two[0]
    swapped_two[...] = slots_two[1]


def add_up(kept, swapped, across, diagonal, *messages):
    for n, message in enumerate(messages):
        message[0] = kept[n] + across[n]
        message[1] = swapped[n] + diagonal[n]


def pair_up(kept, swapped, *messages):
    for n, message in enumerate(messages):
        message[0] = kept[n]
        message[1] = swapped[n]


def pack_other(*refs):
    out = refs[-1]
    there = 1 - (lax.axis_index("grp") & 1)
    for n, ref in enumerate(refs[:-1]):
        out[n] = ref[:, there]


def outer_factors(left_one, middle_one, left_two, middle_two, factors):
    rank = left_one.shape[1]
    factors[:, :rank] = product(left_one[...], middle_one[0, 0])
    factors[:, rank:] = product(left_two[...], middle_two[0, 0])


def combine(factors, *refs):
    levels, (out, stacked) = refs[:-2], refs[-2:]
    me = lax.axis_index("grp")
    quarter = lax.axis_index("quarter")
    core = me & 1
    rank = factors.shape[1] // 2
    quads = (len(levels) - 2) // 4
    straight, diagonal, second = levels[:quads], levels[quads : 2 * quads], levels[2 * quads : -2]
    other_first, other_second = levels[-2:]
    part = other_first.shape[2]

    def put(level, apart, sender, rows):
        row = pl.multiple_of(level * rank + (me ^ (2 * apart + sender)) * part, part)
        stacked[pl.ds(row, part)] = rows

    for sender in range(2):
        for n in range(quads):
            mine, others = 4 * n + 2 * core, 4 * n + 2 * (1 - core)
            put(0, mine + quarter, sender, straight[n][sender, core])
            put(0, mine + 1 - quarter, sender, diagonal[n][sender, core])
            put(0, others + quarter, 1 - sender, other_first[n, sender])
            put(0, others + 1 - quarter, 1 - sender, other_first[quads + n, sender])
        for n in range(2 * quads):
            put(1, 2 * n + core, sender, second[n][sender, core])
            put(1, 2 * n + 1 - core, 1 - sender, other_second[n, sender])
    out[...] = product(factors[...], stacked[...])


def near(mesh, rhs, left_one, left_two, middle_one, middle_two, right_one, right_two, order_one, order_two):
    groups = mesh.shape["grp"]
    chips = groups // 2
    quads = chips // 4
    rank, columns = right_one.shape[1], rhs.shape[1]
    part = rank // groups

    def call(kernel, out_shape, *operands, after=(), cost=None, scratch=()):
        taken = len(operands)

        def body(*refs):
            kernel(*refs[:taken], *refs[taken + len(after) :])

        return pl.pallas_call(
            body,
            out_shape=out_shape,
            in_specs=[HBM if kernel is project else VMEM] * taken + [ANY] * len(after),
            out_specs=jax.tree.map(lambda _: VMEM, out_shape),
            scratch_shapes=scratch,
            compiler_params=PARAMS,
            cost_estimate=cost and pl.CostEstimate(flops=cost, bytes_accessed=cost // 100, transcendentals=0),
        )(*operands, *after)

    def send(value, to):
        sizes = [mesh.shape[axis] for axis in AXES]
        pairs = []
        for h in range(sizes[0]):
            for q in range(sizes[1]):
                for g in range(sizes[2]):
                    a, b, c = to(h, q, g)
                    source = (h * sizes[1] + q) * sizes[2] + g
                    pairs.append((source, (a * sizes[1] + b) * sizes[2] + c))
        return lax.ppermute(value, AXES, pairs)

    def swap_cores(value):
        return send(value, lambda h, q, g: (h, q, g ^ 1))

    def swap_quarters(value):
        return send(value, lambda h, q, g: (h, 1 - q, g))

    message = f32(2, 2, part, columns)
    kept_one, swapped_one, across_one, diagonal_one, kept_two, swapped_two = call(
        project,
        [f32(quads, 2, part, columns)] * 4 + [f32(2 * quads, 2, part, columns)] * 2,
        *(in_hbm(value) for value in (order_one, order_two, rhs, right_one, right_two)),
        scratch=[
            pltpu.VMEM(rhs.shape, jnp.float32),
            pltpu.VMEM((right_one.shape[0], 2 * rank), jnp.float32),
            pltpu.VMEM((2, 2, quads, 2, part, columns), jnp.float32),
            pltpu.VMEM((2, 2 * quads, 2, part, columns), jnp.float32),
            pltpu.SMEM((2, *order_one.shape), jnp.int32),
            pltpu.SemaphoreType.DMA((5,)),
        ],
    )
    across_one = swap_quarters(across_one)
    diagonal_one = send(diagonal_one, lambda h, q, g: (h, 1 - q, g ^ 1))
    swapped_two = swap_cores(swapped_two)
    swapped_one = swap_cores(swapped_one)
    messages_two = call(
        pair_up, [message] * (2 * quads), kept_two, swapped_two, after=(swapped_one,)
    )
    second = [
        send(messages_two[n], lambda h, q, g, n=n: (h, 1 - q, g ^ (2 * (2 * n + g % 2))))
        for n in range(2 * quads)
    ]
    messages_one = call(
        add_up,
        [message] * quads,
        *(kept_one, swapped_one, across_one, diagonal_one),
        after=(messages_two[0],),
        cost=COST,
    )
    straight, diagonal = (
        [
            send(
                messages_one[n],
                lambda h, q, g, n=n: (1 - h, q ^ other, g ^ (2 * (4 * n + 2 * (g % 2) + q))),
            )
            for n in range(quads)
        ]
        for other in range(2)
    )
    other_second = swap_cores(call(pack_other, f32(2 * quads, 2, part, columns), *second))
    other_first = swap_cores(call(pack_other, f32(2 * quads, 2, part, columns), *straight, *diagonal, after=(other_second,)))
    factors = call(
        outer_factors, f32(left_one.shape[0], 2 * rank), left_one, middle_one, left_two, middle_two
    )
    return call(
        combine,
        f32(left_one.shape[0], columns),
        *(factors, *straight, *diagonal, *second, other_first, other_second),
        scratch=[pltpu.VMEM((2 * rank, columns), jnp.float32)],
    )


def project_far(order_one, order_two, rhs, right_one, right_two, slots_one, slots_two):
    part = slots_one.shape[1]
    levels = ((order_one, right_one, slots_one), (order_two, right_two, slots_two))
    for order, right, slots in levels:
        coeffs = product(right[...], rhs[...], ((0,), (0,)))
        for p in range(order.shape[2]):
            slots[order[0, 0, p]] = coeffs[p * part : (p + 1) * part]


def far(mesh, rhs, left_one, left_two, middle_one, middle_two, right_one, right_two, order_one, order_two):
    groups = mesh.shape["grp"]
    rank, columns = right_one.shape[1], rhs.shape[1]
    slots = pl.pallas_call(
        project_far,
        out_shape=[f32(groups, rank // groups, columns)] * 2,
        in_specs=[SMEM, SMEM, VMEM, VMEM, VMEM],
        out_specs=[VMEM, VMEM],
        compiler_params=PARAMS,
    )(order_one, order_two, rhs, right_one, right_two)
    swap = [(0, 1), (1, 0)]
    first, second = (
        lax.all_to_all(value, "grp", 0, 0, tiled=True).reshape(rank, columns) for value in slots
    )
    first = lax.ppermute(first, "half", swap)
    first = first + lax.ppermute(first, "quarter", swap)
    second = lax.ppermute(second, "quarter", swap)
    dot = functools.partial(jnp.dot, precision=lax.Precision.HIGHEST)
    result = dot(left_one, dot(middle_one[0, 0], first))
    return result + dot(left_two, dot(middle_two[0, 0], second))


def solution(mesh):
    in_specs = (
        P(AXES, None),
        P(AXES, None),
        P(AXES, None),
        P("half", "grp", None, None),
        P(("half", "quarter"), "grp", None, None),
        P(AXES, None),
        P(AXES, None),
        P("half", "grp", None),
        P(("half", "quarter"), "grp", None),
    )
    groups = mesh.shape["grp"]
    direct = groups >= 8 and groups & (groups - 1) == 0 and groups // 2 <= MOST_CHIPS
    return jax.shard_map(
        functools.partial(near if direct else far, mesh),
        mesh=mesh,
        in_specs=in_specs,
        out_specs=P(AXES, None),
        check_vma=False,
    )
```

```python
import functools

import jax
import jax.numpy as jnp
from jax import lax
from jax.experimental import pallas as pl
from jax.experimental.pallas import tpu as pltpu
from jax.sharding import PartitionSpec as P

AXES = ("half", "quarter", "grp")
MOST_CHIPS = 8
COST = 10**10
TABLE = ((3, 1), (0, 2))
COLUMN_BLOCKS = 1
PARAMS = pltpu.CompilerParams(vmem_limit_bytes=16 * 2**20)
VMEM = pl.BlockSpec(memory_space=pltpu.VMEM)
ANY = pl.BlockSpec(memory_space=pl.ANY)
HBM = pl.BlockSpec(memory_space=pltpu.HBM)
SMEM = pl.BlockSpec(memory_space=pltpu.SMEM)


def f32(*shape):
    return jax.ShapeDtypeStruct(shape, jnp.float32)


def in_hbm(value):
    return pltpu.with_memory_space_constraint(value, pltpu.HBM)


def split(value):
    high = value.astype(jnp.bfloat16)
    low = (value - high.astype(jnp.float32)).astype(jnp.bfloat16)
    return high, low


def product(left, right):
    dot = functools.partial(jnp.dot, preferred_element_type=jnp.float32)
    (lh, ll), (rh, rl) = left, split(right)
    return dot(lh, rh) + (dot(lh, rl) + dot(ll, rh))


def project(
    order_one, order_two, rhs, right_one, right_two,
    kept_one, swapped_one, across_one, diagonal_one, kept_two, swapped_two,
    values, rights, slots_one, slots_two, orders, sems,
):
    rank = right_one.shape[1]
    pairs = (
        (right_one, rights.at[:, :rank]),
        (right_two, rights.at[:, rank:]),
        (order_one, orders.at[0]),
        (order_two, orders.at[1]),
    )
    width = rhs.shape[1] // COLUMN_BLOCKS
    blocks = [pl.ds(n * width, width) for n in range(COLUMN_BLOCKS)]
    pairs += tuple((rhs.at[:, block], values.at[:, block]) for block in blocks)
    copies = [pltpu.make_async_copy(*pair, sems.at[n]) for n, pair in enumerate(pairs)]
    for copy in copies:
        copy.start()
    me = lax.axis_index("grp")
    quarter = lax.axis_index("quarter")
    for copy in copies[:4]:
        copy.wait()
    left = split(rights[...].T)
    part = slots_one.shape[4]
    for copy, block in zip(copies[4:], blocks):
        copy.wait()
        coeffs = product(left, values[:, block])
        for p in range(rank // part):
            first, second = (
                coeffs[n * rank + p * part : n * rank + (p + 1) * part] for n in range(2)
            )
            receiver = orders[0, 0, 0, p]
            apart = (receiver >> 1) ^ (me >> 1)
            core = ((apart >> 1) ^ me) & 1
            slots_one[core, (apart ^ quarter) & 1, apart >> 2, receiver & 1, :, block] = first
            receiver = orders[1, 0, 0, p]
            apart = (receiver >> 1) ^ (me >> 1)
            core, place = 0, 0
            for c in range(2):
                for m in range(2):
                    core = jnp.where((apart & 3) == TABLE[c][m], c, core)
                    place = jnp.where((apart & 3) == TABLE[c][m], m, place)
            slots_two[(core ^ me) & 1, (apart >> 2) * 2 + place, receiver & 1, :, block] = second
    kept_one[...] = slots_one[0, 0]
    swapped_one[...] = slots_one[1, 0]
    across_one[...] = slots_one[0, 1]
    diagonal_one[...] = slots_one[1, 1]
    kept_two[...] = slots_two[0]
    swapped_two[...] = slots_two[1]


def add_up(kept, swapped, across, diagonal, *messages):
    for n, message in enumerate(messages):
        message[0] = kept[n] + across[n]
        message[1] = swapped[n] + diagonal[n]


def pair_up(kept, swapped, *messages):
    for n, message in enumerate(messages):
        message[0] = kept[n]
        message[1] = swapped[n]


def pack_other(*refs):
    out = refs[-1]
    there = 1 - (lax.axis_index("grp") & 1)
    for n, ref in enumerate(refs[:-1]):
        out[n] = ref[:, there]


def outer_factors(left_one, middle_one, left_two, middle_two, factors):
    rank = left_one.shape[1]
    factors[:, :rank] = product(split(left_one[...]), middle_one[0, 0])
    factors[:, rank:] = product(split(left_two[...]), middle_two[0, 0])


def combine(factors, *refs):
    levels, (out, stacked) = refs[:-2], refs[-2:]
    me = lax.axis_index("grp")
    quarter = lax.axis_index("quarter")
    core = me & 1
    rank = factors.shape[1] // 2
    quads = (len(levels) - 2) // 4
    straight, diagonal, second = levels[:quads], levels[quads : 2 * quads], levels[2 * quads : -2]
    other_first, other_second = levels[-2:]
    part = other_first.shape[2]

    def put(level, apart, sender, rows):
        row = pl.multiple_of(level * rank + (me ^ (2 * apart + sender)) * part, part)
        stacked[pl.ds(row, part)] = rows

    for sender in range(2):
        for n in range(quads):
            mine, others = 4 * n + 2 * core, 4 * n + 2 * (1 - core)
            put(0, mine + quarter, sender, straight[n][sender, core])
            put(0, mine + 1 - quarter, sender, diagonal[n][sender, core])
            put(0, others + quarter, 1 - sender, other_first[n, sender])
            put(0, others + 1 - quarter, 1 - sender, other_first[quads + n, sender])
        for n in range(2 * quads):
            here, there = (
                4 * (n // 2) + jnp.where(core == c, TABLE[1][n % 2], TABLE[0][n % 2]) for c in (1, 0)
            )
            put(1, here, sender, second[n][sender, core])
            put(1, there, 1 - sender, other_second[n, sender])
    out[...] = product(split(factors[...]), stacked[...])


def near(mesh, rhs, left_one, left_two, middle_one, middle_two, right_one, right_two, order_one, order_two):
    groups = mesh.shape["grp"]
    chips = groups // 2
    quads = chips // 4
    rank, columns = right_one.shape[1], rhs.shape[1]
    part = rank // groups

    def call(kernel, out_shape, *operands, after=(), cost=None, scratch=()):
        taken = len(operands)

        def body(*refs):
            kernel(*refs[:taken], *refs[taken + len(after) :])

        return pl.pallas_call(
            body,
            out_shape=out_shape,
            in_specs=[HBM if kernel is project else VMEM] * taken + [ANY] * len(after),
            out_specs=jax.tree.map(lambda _: VMEM, out_shape),
            scratch_shapes=scratch,
            compiler_params=PARAMS,
            cost_estimate=cost and pl.CostEstimate(flops=cost, bytes_accessed=cost // 100, transcendentals=0),
        )(*operands, *after)

    def send(value, to):
        sizes = [mesh.shape[axis] for axis in AXES]
        pairs = []
        for h in range(sizes[0]):
            for q in range(sizes[1]):
                for g in range(sizes[2]):
                    a, b, c = to(h, q, g)
                    source = (h * sizes[1] + q) * sizes[2] + g
                    pairs.append((source, (a * sizes[1] + b) * sizes[2] + c))
        return lax.ppermute(value, AXES, pairs)

    def swap_cores(value):
        return send(value, lambda h, q, g: (h, q, g ^ 1))

    def swap_quarters(value):
        return send(value, lambda h, q, g: (h, 1 - q, g))

    message = f32(2, 2, part, columns)
    kept_one, swapped_one, across_one, diagonal_one, kept_two, swapped_two = call(
        project,
        [f32(quads, 2, part, columns)] * 4 + [f32(2 * quads, 2, part, columns)] * 2,
        *(in_hbm(value) for value in (order_one, order_two, rhs, right_one, right_two)),
        scratch=[
            pltpu.VMEM(rhs.shape, jnp.float32),
            pltpu.VMEM((right_one.shape[0], 2 * rank), jnp.float32),
            pltpu.VMEM((2, 2, quads, 2, part, columns), jnp.float32),
            pltpu.VMEM((2, 2 * quads, 2, part, columns), jnp.float32),
            pltpu.SMEM((2, *order_one.shape), jnp.int32),
            pltpu.SemaphoreType.DMA((4 + COLUMN_BLOCKS,)),
        ],
    )
    across_one = swap_quarters(across_one)
    diagonal_one = send(diagonal_one, lambda h, q, g: (h, 1 - q, g ^ 1))
    swapped_two = swap_cores(swapped_two)
    swapped_one = swap_cores(swapped_one)
    messages_two = call(
        pair_up, [message] * (2 * quads), kept_two, swapped_two, after=(swapped_one,)
    )
    second = [
        send(messages_two[n], lambda h, q, g, n=n: (h, 1 - q, g ^ (2 * (4 * (n // 2) + TABLE[g % 2][n % 2]))))
        for n in range(2 * quads)
    ]
    messages_one = call(
        add_up,
        [message] * quads,
        *(kept_one, swapped_one, across_one, diagonal_one),
        after=(messages_two[0],),
        cost=COST,
    )
    straight, diagonal = (
        [
            send(
                messages_one[n],
                lambda h, q, g, n=n: (1 - h, q ^ other, g ^ (2 * (4 * n + 2 * (g % 2) + q))),
            )
            for n in range(quads)
        ]
        for other in range(2)
    )
    other_second = swap_cores(call(pack_other, f32(2 * quads, 2, part, columns), *second))
    other_first = swap_cores(call(pack_other, f32(2 * quads, 2, part, columns), *straight, *diagonal, after=(other_second,)))
    factors = call(
        outer_factors, f32(left_one.shape[0], 2 * rank), left_one, middle_one, left_two, middle_two
    )
    return call(
        combine,
        f32(left_one.shape[0], columns),
        *(factors, *straight, *diagonal, *second, other_first, other_second),
        scratch=[pltpu.VMEM((2 * rank, columns), jnp.float32)],
    )


def project_far(order_one, order_two, rhs, right_one, right_two, slots_one, slots_two):
    part = slots_one.shape[1]
    levels = ((order_one, right_one, slots_one), (order_two, right_two, slots_two))
    for order, right, slots in levels:
        coeffs = product(split(right[...].T), rhs[...])
        for p in range(order.shape[2]):
            slots[order[0, 0, p]] = coeffs[p * part : (p + 1) * part]


def far(mesh, rhs, left_one, left_two, middle_one, middle_two, right_one, right_two, order_one, order_two):
    groups = mesh.shape["grp"]
    rank, columns = right_one.shape[1], rhs.shape[1]
    slots = pl.pallas_call(
        project_far,
        out_shape=[f32(groups, rank // groups, columns)] * 2,
        in_specs=[SMEM, SMEM, VMEM, VMEM, VMEM],
        out_specs=[VMEM, VMEM],
        compiler_params=PARAMS,
    )(order_one, order_two, rhs, right_one, right_two)
    swap = [(0, 1), (1, 0)]
    first, second = (
        lax.all_to_all(value, "grp", 0, 0, tiled=True).reshape(rank, columns) for value in slots
    )
    first = lax.ppermute(first, "half", swap)
    first = first + lax.ppermute(first, "quarter", swap)
    second = lax.ppermute(second, "quarter", swap)
    dot = functools.partial(jnp.dot, precision=lax.Precision.HIGHEST)
    result = dot(left_one, dot(middle_one[0, 0], first))
    return result + dot(left_two, dot(middle_two[0, 0], second))


def solution(mesh):
    in_specs = (
        P(AXES, None),
        P(AXES, None),
        P(AXES, None),
        P("half", "grp", None, None),
        P(("half", "quarter"), "grp", None, None),
        P(AXES, None),
        P(AXES, None),
        P("half", "grp", None),
        P(("half", "quarter"), "grp", None),
    )
    groups = mesh.shape["grp"]
    direct = groups >= 8 and groups & (groups - 1) == 0 and groups // 2 <= MOST_CHIPS
    return jax.shard_map(
        functools.partial(near if direct else far, mesh),
        mesh=mesh,
        in_specs=in_specs,
        out_specs=P(AXES, None),
        check_vma=False,
    )
```
